512 devices in a mesh: grp: 16 (over y, x_lo, core), seq: 32 (over x_hi, z).
Axes of the slice: x: 4 (x_hi: 2, x_lo: 2; x = x_hi * 2 + x_lo), y: 4, z: 16, core: 2. Of those that a mesh axis runs over, the one named last changes fastest.
Arguments:
- query_heads: bfloat16 [128, 12, 512, 128], P('grp', None, 'seq'), may hold values from -40 to 40
- key_heads: bfloat16 [128, 12, 512, 128], P('grp', None, 'seq'), may hold values from -40 to 40
- value_heads: bfloat16 [128, 12, 512, 128], P('grp', None, 'seq'), may hold values from -8 to 8
- residual: bfloat16 [128, 512, 1536], P('grp', 'seq'), may hold values from -16 to 16
- modulation: bfloat16 [128, 4, 1536], P('grp'), may hold values from 0.099609375 to 1.8984375
- router: bfloat16 [1536, 32], replicated, may hold values from -0.15625 to 0.15625
- up_proj: bfloat16 [32, 2048, 1536], P('seq', 'grp'), may hold values from -0.15625 to 0.15625
- down_proj: bfloat16 [32, 2048, 1536], P('seq', 'grp'), may hold values from -0.125 to 0.125
- expert_ids: int32 [16, 32, 128, 2], P('grp', 'seq'), may hold values from 0 to 31, all different within a row; in each aligned block of 128 rows (0 to 127, 128 to 255, ..., all dimensions but the last counted through in order) at most 16 rows name the same one
Outputs:
- output: bfloat16 [128, 512, 1536], P('grp', 'seq')
The draws below stay inside these ranges and needn't reach their ends.
Inputs may be any that keep to these rules, and one draw needn't show every extreme that they name: `expert_ids`: each token names two different experts. Among the 128 tokens of one device no expert is named by more than 16 of them, and in every draw some device names some expert exactly 16 times.
All inputs are finite; a program needn't handle non-finite values.
Results may differ from the reference program's by a relative error of at most 0.012.
Values may be sent and summed in bfloat16 or wider, within the bound.
No kernel may reach another device: no remote copies, remote signals or barrier semaphores. Data moves between devices by JAX's collectives and lax.ppermute only.
A program may use at most 64 MiB of HBM per device.

```python
import math
import jax
import jax.numpy as jnp
import numpy as np
from jax import lax

HEAD_DIM = 128
HEADS = 12
D = 1536
FF = 2048
SEQS = 8
LD = 16
EXPERTS = 32
TOK_DEV = 128
LENGTH = 512
BATCH = 128
C = 16
N_GRP = 16
N_SEQ = 32


def paired_fields(key):
    dims_all = (BATCH, HEADS, LENGTH, HEAD_DIM)
    return dims_all


def draw_query_heads(key, part):
    dims_all = paired_fields(key)
    key = jax.random.fold_in(key, 1)
    field = 1.3 * jax.random.normal(key, dims_all, jnp.float32)
    return jnp.clip(field, -40.0, 40.0).astype(jnp.bfloat16)


def draw_key_heads(key, part):
    dims_all = paired_fields(key)
    key = jax.random.fold_in(key, 2)
    field = 1.3 * jax.random.normal(key, dims_all, jnp.float32)
    return jnp.clip(field, -40.0, 40.0).astype(jnp.bfloat16)


def draw_residual(key, part):
    key = jax.random.fold_in(key, 3)
    dims_all = (BATCH, LENGTH, D)
    field = jax.random.normal(key, dims_all, jnp.float32)
    return jnp.clip(field, -16.0, 16.0).astype(jnp.bfloat16)


def block_levels(stream_key, dims, shards, smallest, high):
    level = 1.0
    for dim, parts in shards:
        steps = jax.random.uniform(jax.random.fold_in(jax.random.fold_in(stream_key, 6), dim), (parts,), jnp.float32, smallest / len(shards), high / len(shards))
        level = level * jnp.repeat(jnp.exp(steps), dims[dim] // parts).reshape((-1,) + (1,) * (len(dims) - 1 - dim))
    return level


def routed_block(own_key, own, number, rows, amount, top, limit, skew):
    sequence = jax.random.permutation(own_key, amount)
    crowded, usual = shares(amount, rows * top, limit, skew, True), shares(amount, rows * top, limit, skew, False)
    places = jnp.arange(amount)

    def named(lengths, offset_by):
        used = int((lengths > 0).sum())
        fixed = max(1, used // 4)
        moved = fixed + (places - fixed + offset_by * (used - fixed)) % max(1, amount - fixed)
        return jnp.zeros((amount,), jnp.int32).at[sequence[jnp.where(places < fixed, places, moved)]].set(jnp.asarray(lengths, jnp.int32))

    lengths = jnp.where(number % 4 == 0, named(crowded, number // 4), named(usual, number - number // 4 - 1))
    mixed = jax.random.permutation(jax.random.fold_in(own, 3), amount)
    source_of, taker = mixed[0:amount // 2 * 2:2], mixed[1:amount // 2 * 2:2]
    room = jnp.minimum(lengths[source_of] - 1, limit - lengths[taker]) // 2
    room = jnp.where((source_of == sequence[0]) | (taker == sequence[0]) | (lengths[taker] == 0), 0, jnp.maximum(room, 0))
    moved = jax.random.randint(jax.random.fold_in(own, 4), (amount // 2,), 0, 1 << 20) % (room + 1)
    lengths = lengths.at[source_of].add(-moved).at[taker].add(moved)
    items = jnp.searchsorted(jnp.cumsum(lengths), jnp.arange(rows * top), side="right").astype(jnp.int32)
    grid = items.reshape(top, rows).T
    grid = grid[jax.random.permutation(jax.random.fold_in(own, 1), rows)]
    offset_by = jax.random.randint(jax.random.fold_in(own, 2), (rows, 1), 0, top)
    return jnp.take_along_axis(grid, (jnp.arange(top)[None, :] + offset_by) % top, axis=1)


def shares(count, total, limit, skew, full):
    loads = [(1 << 20) // math.isqrt(grade ** skew) + 1 for grade in range(1, count + 1)]
    largest = limit if full else min(limit, max(-(-total // count), total * loads[0] // sum(loads)))
    least = 1 if total - largest >= count - 1 else 0
    holding, surplus = [largest] + [least] * (count - 1), total - largest - least * (count - 1)
    while surplus > 0:
        movable = [i for i in range(1, count) if holding[i] < largest] or [i for i in range(1, count) if holding[i] < limit]
        whole, remaining = sum([loads[i] for i in movable]), surplus
        for i in movable:
            addition = min(limit - holding[i], max(1, remaining * loads[i] // whole), surplus)
            holding[i] = holding[i] + addition
            surplus = surplus - addition
    return np.array(holding)


def normal_values(own_key, dims, width, reach, cuts=(), kind=jnp.bfloat16):
    gain = block_levels(own_key, dims, cuts, -0.22, 0.18) if cuts else 1.0
    entries = jax.random.normal(own_key, dims, jnp.float32) * width * gain
    return jnp.minimum(jnp.maximum(entries, -reach), reach).astype(kind)


def setup_inputs(seed: int = 0) -> dict:
    key_list = jax.random.split(jax.random.key(seed), 10)
    query_heads = draw_query_heads(jax.random.fold_in(key_list[9], 71), 0)
    key_heads = draw_key_heads(jax.random.fold_in(key_list[9], 71), 0)
    value_heads = normal_values(key_list[2], (BATCH, HEADS, LENGTH, HEAD_DIM), 2.0, 8.0, ((0, 16), (2, 32)))
    residual = draw_residual(jax.random.fold_in(key_list[9], 71), 0)
    modulation = jnp.clip(1.0 + 0.18 * jax.random.normal(key_list[4], (BATCH, 4, D), jnp.float32), 0.099609375, 1.8984375).astype(jnp.bfloat16)
    router = normal_values(key_list[5], (D, EXPERTS), D ** -0.5, 0.15625)
    up_proj = normal_values(key_list[6], (EXPERTS, FF, D), D ** -0.5, 0.15625, ((0, 32), (1, 16)))
    down_proj = normal_values(key_list[7], (EXPERTS, FF, D), FF ** -0.5, 0.125, ((0, 32), (1, 16)))
    expert_ids_keys = jax.random.split(jax.random.fold_in(key_list[8], 1), N_GRP * N_SEQ * TOK_DEV // TOK_DEV)
    expert_ids_turns = jax.random.permutation(jax.random.fold_in(key_list[8], 3), N_GRP * N_SEQ * TOK_DEV // TOK_DEV)
    expert_ids = jax.vmap(lambda own, number: routed_block(jax.random.fold_in(key_list[8], 2), own, number, TOK_DEV, EXPERTS, 2, C, 2))(expert_ids_keys, expert_ids_turns).reshape((N_GRP, N_SEQ, TOK_DEV, 2))
    return {"query_heads": query_heads, "key_heads": key_heads, "value_heads": value_heads, "residual": residual, "modulation": modulation, "router": router, "up_proj": up_proj, "down_proj": down_proj, "expert_ids": expert_ids}


norm_eps = 1e-06

def attend_sequence(pieces):
    single_query_rows, single_key_rows, single_value_rows = pieces
    scale_factor_term = 1.0 / math.sqrt(single_query_rows.shape[-1])
    attention_scores = jnp.einsum('nrf,njf->nrj', single_query_rows.astype(jnp.float32), single_key_rows.astype(jnp.float32)) * scale_factor_term
    weight_matrix_set = jax.nn.softmax(attention_scores, axis=-1).astype(jnp.bfloat16)
    return jnp.einsum('xob,xbp->xop', weight_matrix_set.astype(jnp.float32), single_value_rows.astype(jnp.float32)).astype(jnp.bfloat16)

def reference(query_heads, key_heads, value_heads, residual, modulation, router, up_proj, down_proj, expert_ids):
    batch_size, head_count, length, head_width = query_heads.shape
    model_width = head_count * head_width
    attended = lax.map(attend_sequence, (query_heads, key_heads, value_heads))
    attn_tok = attended.transpose(0, 2, 1, 3).reshape(batch_size, length, model_width)
    modulators = modulation.astype(jnp.float32)
    stream = (residual.astype(jnp.float32) + modulators[:, 0:1, :] * attn_tok.astype(jnp.float32)).astype(jnp.bfloat16)
    widened = stream.astype(jnp.float32)
    center = lax.optimization_barrier(jnp.mean(widened, axis=-1, keepdims=True))
    spread = lax.optimization_barrier(jnp.mean(jnp.square(widened - center), axis=-1, keepdims=True))
    normed = ((widened - center) * lax.rsqrt(spread + norm_eps) * modulators[:, 1:2, :] + modulators[:, 2:3, :]).astype(jnp.bfloat16)
    token_count = batch_size * length
    tokens = normed.reshape(token_count, model_width)
    chosen = expert_ids.reshape(N_GRP, N_SEQ, SEQS, LD, 2).transpose(0, 2, 1, 3, 4).reshape(token_count, 2).astype(jnp.int32)
    logits = jnp.dot(tokens, router, preferred_element_type=jnp.float32)
    picked = jnp.take_along_axis(logits, chosen, axis=1)
    lifted = jax.nn.sigmoid(picked)
    gate_mix = lifted / lax.optimization_barrier(jnp.sum(lifted, axis=1, keepdims=True))
    experts = router.shape[1]
    assign_expert = chosen.reshape(-1)
    assign_token = (jnp.arange(token_count * 2, dtype=jnp.int32) // 2).astype(jnp.int32)
    assign_gate = gate_mix.reshape(-1)
    sorted_ids = jnp.argsort(assign_expert, stable=True).astype(jnp.int32)
    counts = lax.optimization_barrier(jnp.sum((assign_expert[:, None] == jnp.arange(experts, dtype=jnp.int32)[None, :]).astype(jnp.int32), axis=0))
    offsets = (jnp.cumsum(counts) - counts).astype(jnp.int32)
    block_rows = 512
    padded_ids = jnp.concatenate([sorted_ids, jnp.zeros((block_rows,), jnp.int32)])

    def one_expert(running, expert_index):
        up_mat = up_proj[expert_index]
        down_mat = down_proj[expert_index]
        first_row = offsets[expert_index]
        live_count = counts[expert_index]

        def one_block(block_step, inner_total):
            row_begin = (first_row + block_step * block_rows).astype(jnp.int32)
            picked_rows = lax.dynamic_slice(padded_ids, (row_begin,), (block_rows,))
            active_flag = block_step * block_rows + jnp.arange(block_rows, dtype=jnp.int32) < live_count
            token_index = assign_token[picked_rows]
            gathered = tokens[token_index]
            pre_act = lax.dot_general(gathered, up_mat, (((1,), (1,)), ((), ())), preferred_element_type=jnp.float32)
            hidden = jax.nn.gelu(pre_act).astype(jnp.bfloat16)
            result = jnp.dot(hidden, down_mat, preferred_element_type=jnp.float32).astype(jnp.bfloat16)
            weight = jnp.where(active_flag, assign_gate[picked_rows], jnp.zeros_like(assign_gate[picked_rows]))
            return inner_total.at[token_index].add(weight[:, None] * result.astype(jnp.float32))
        block_total = ((live_count + block_rows - 1) // block_rows).astype(jnp.int32)
        running = lax.fori_loop(jnp.int32(0), block_total, one_block, running)
        return (running, None)
    moe_sum, _ = lax.scan(one_expert, jnp.zeros((token_count, model_width), jnp.float32), jnp.arange(experts, dtype=jnp.int32))
    moe_sum = moe_sum.reshape(batch_size, length, model_width)
    return (widened + modulators[:, 3:4, :] * moe_sum).astype(jnp.bfloat16)
```

```python
import math

import jax
import jax.numpy as jnp
from jax import lax
from jax.experimental import pallas as pl
from jax.experimental.pallas import tpu as pltpu
from jax.sharding import PartitionSpec as P

norm_eps = 1e-06
f32 = jnp.float32
bf16 = jnp.bfloat16


def attention_kernel(q_ref, k_ref, v_ref, o_ref):
    blocks, _, rows, width = q_ref.shape
    length = blocks * rows
    scale = 1.0 / math.sqrt(width)
    q = q_ref[...].reshape(length, width)
    k = k_ref[...].reshape(length, width)
    v = v_ref[...].reshape(length, width)
    scores = lax.dot_general(q, k, (((1,), (1,)), ((), ())), preferred_element_type=f32)
    top = jnp.max(scores, axis=1, keepdims=True)
    powers = jnp.exp((scores - top) * scale)
    total = jnp.sum(powers, axis=1, keepdims=True)
    weights = (powers * (1.0 / total)).astype(bf16)
    out = jnp.dot(weights, v, preferred_element_type=f32).astype(bf16)
    o_ref[...] = out.reshape(blocks, 1, rows, width)


def attend(qkv):
    blocks, triple, rows, width = qkv.shape
    pairs = triple // 3

    def spec(first):
        return pl.BlockSpec((blocks, 1, rows, width), lambda i: (0, first + i, 0, 0))

    length = blocks * rows
    return pl.pallas_call(
        attention_kernel,
        grid=(pairs,),
        in_specs=[spec(0), spec(pairs), spec(2 * pairs)],
        out_specs=spec(0),
        out_shape=jax.ShapeDtypeStruct((blocks, pairs, rows, width), bf16),
        compiler_params=pltpu.CompilerParams(vmem_limit_bytes=32 * 2**20),
        cost_estimate=pl.CostEstimate(
            flops=4 * pairs * length * length * width,
            bytes_accessed=8 * pairs * length * width,
            transcendentals=pairs * length * length,
        ),
        name="attend",
    )(qkv, qkv, qkv)


def choices(ids, experts):
    tokens = ids.shape[0]
    lanes = lax.broadcasted_iota(jnp.int32, (tokens, experts), 1)
    first = (lanes == ids[:, 0:1]).astype(f32)
    second = (lanes == ids[:, 1:2]).astype(f32)
    below = (
        lax.broadcasted_iota(jnp.int32, (tokens, tokens), 0)
        > lax.broadcasted_iota(jnp.int32, (tokens, tokens), 1)
    ).astype(bf16)
    before = jnp.dot(below, (first + second).astype(bf16), preferred_element_type=f32)
    capacity = 4 * tokens // experts
    out = []
    for k, onehot in enumerate((first, second)):
        slot = jnp.sum(before * onehot, axis=1, keepdims=True).astype(jnp.int32)
        out.append((onehot, ids[:, k : k + 1] * capacity + slot))
    return out


def placing(target, slots):
    tokens = target.shape[0]
    lanes = lax.broadcasted_iota(jnp.int32, (tokens, slots), 1)
    return (lanes == target).astype(f32).astype(bf16)


def route_kernel(attn_ref, res_ref, mod_ref, router_ref, ids_ref, stream_ref, out_ref, gate_ref, tok_ref):
    seqs, heads, rows, width = attn_ref.shape
    experts = router_ref.shape[1]
    for b in range(seqs):
        attn = jnp.concatenate([attn_ref[b, h].astype(f32) for h in range(heads)], axis=1)
        mod = mod_ref[b].astype(f32)
        stream = (res_ref[b].astype(f32) + mod[0:1] * attn).astype(bf16)
        stream_ref[b * rows : (b + 1) * rows, :] = stream
        wide = stream.astype(f32)
        center = jnp.mean(wide, axis=1, keepdims=True)
        moved = wide - center
        spread = jnp.mean(moved * moved, axis=1, keepdims=True)
        tok_ref[b * rows : (b + 1) * rows, :] = (
            moved * lax.rsqrt(spread + norm_eps) * mod[1:2] + mod[2:3]
        ).astype(bf16)
    tokens = tok_ref[...]
    logits = jnp.dot(tokens, router_ref[...], preferred_element_type=f32)
    picks = choices(ids_ref[...], experts)
    gates = [jax.nn.sigmoid(jnp.sum(onehot * logits, axis=1, keepdims=True)) for onehot, _ in picks]
    total = gates[0] + gates[1]
    gate_ref[...] = jnp.concatenate([gates[0] / total, gates[1] / total], axis=1)
    slots = out_ref.shape[0]
    place = placing(picks[0][1], slots) + placing(picks[1][1], slots)
    out_ref[...] = lax.dot_general(
        place, tokens, (((0,), (0,)), ((), ())), preferred_element_type=f32
    ).astype(bf16)


def route(attn, residual, modulation, router, ids):
    tokens = ids.shape[0]
    model_width = residual.shape[-1]
    slots = 4 * tokens
    return pl.pallas_call(
        route_kernel,
        out_shape=(
            jax.ShapeDtypeStruct((tokens, model_width), bf16),
            jax.ShapeDtypeStruct((slots, model_width), bf16),
            jax.ShapeDtypeStruct((tokens, 2), f32),
        ),
        scratch_shapes=[pltpu.VMEM((tokens, model_width), bf16)],
        compiler_params=pltpu.CompilerParams(vmem_limit_bytes=32 * 2**20),
        name="route",
    )(attn, residual, modulation, router, ids)


def combine_kernel(back_ref, stream_ref, mod_ref, gate_ref, ids_ref, out_ref, *, experts):
    seqs, rows, _ = out_ref.shape
    picks = choices(ids_ref[...], experts)
    slots = back_ref.shape[0]
    back = back_ref[...]
    moe = None
    for k in range(2):
        part = gate_ref[:, k : k + 1] * jnp.dot(
            placing(picks[k][1], slots), back, preferred_element_type=f32
        )
        moe = part if moe is None else moe + part
    for b in range(seqs):
        span = slice(b * rows, (b + 1) * rows)
        out_ref[b] = (
            stream_ref[span, :].astype(f32) + mod_ref[b, 3:4].astype(f32) * moe[span, :]
        ).astype(bf16)


def combine(back, stream, modulation, gates, ids, experts, rows):
    def kernel(*refs):
        combine_kernel(*refs, experts=experts)

    seqs = modulation.shape[0]
    return pl.pallas_call(
        kernel,
        out_shape=jax.ShapeDtypeStruct((seqs, rows, stream.shape[1]), bf16),
        compiler_params=pltpu.CompilerParams(vmem_limit_bytes=32 * 2**20),
        name="combine",
    )(back, stream, modulation, gates, ids)


def swap(blocks):
    return lax.all_to_all(blocks, "seq", split_axis=0, concat_axis=0, tiled=True)


def per_device(
    query_heads,
    key_heads,
    value_heads,
    residual,
    modulation,
    router,
    up_proj,
    down_proj,
    expert_ids,
):
    seqs_dev, head_count, len_dev, head_width = query_heads.shape
    group_indices = lax.axis_size("seq")
    pair_count = seqs_dev * head_count // group_indices
    tok_dev = seqs_dev * len_dev
    model_width = head_count * head_width
    experts = router.shape[1]
    capacity = 4 * tok_dev // experts
    ids = expert_ids.reshape(tok_dev, 2)

    up_piece = lax.all_gather(up_proj[0], "grp", axis=0, tiled=True)
    down_piece = lax.all_gather(down_proj[0], "grp", axis=0, tiled=True)

    def arrange(array):
        return array.reshape(group_indices, pair_count, len_dev, head_width)

    def together(*arrays):
        return swap(jnp.concatenate(arrays, axis=1))

    def apart(*arrays):
        return jnp.concatenate([swap(array) for array in arrays], axis=1)

    core = lax.axis_index("grp") % 2
    qkv = lax.cond(
        core == 0, together, apart, arrange(query_heads), arrange(key_heads), arrange(value_heads)
    )
    attn = swap(attend(qkv)).reshape(seqs_dev, head_count, len_dev, head_width)
    stream, outbound, gates = route(attn, residual, modulation, router, ids)
    arrived = swap(outbound.reshape(experts, capacity, model_width)).reshape(
        group_indices * capacity, model_width
    )
    pre_act = lax.dot_general(
        arrived, up_piece, (((1,), (1,)), ((), ())), preferred_element_type=f32
    )
    hidden = jax.nn.gelu(pre_act).astype(bf16)
    results = jnp.dot(hidden, down_piece, preferred_element_type=f32).astype(bf16)
    back = swap(results.reshape(group_indices, capacity, model_width)).reshape(
        experts * capacity, model_width
    )
    return combine(back, stream, modulation, gates, ids, experts, len_dev)


def solution(mesh):
    return jax.shard_map(
        per_device,
        mesh=mesh,
        in_specs=(
            P("grp", None, "seq", None),
            P("grp", None, "seq", None),
            P("grp", None, "seq", None),
            P("grp", "seq", None),
            P("grp", None, None),
            P(),
            P("seq", "grp", None),
            P("seq", "grp", None),
            P("grp", "seq", None, None),
        ),
        out_specs=P("grp", "seq", None),
        check_vma=False,
    )
```

```python
import math

import jax
import jax.numpy as jnp
from jax import lax
from jax.experimental import pallas as pl
from jax.experimental.pallas import tpu as pltpu
from jax.sharding import PartitionSpec as P

norm_eps = 1e-06
f32 = jnp.float32
bf16 = jnp.bfloat16


def attention_kernel(q_ref, k_ref, v_ref, o_ref):
    blocks, _, rows, width = q_ref.shape
    length = blocks * rows
    scale = 1.0 / math.sqrt(width)
    q = q_ref[...].reshape(length, width)
    k = k_ref[...].reshape(length, width)
    v = v_ref[...].reshape(length, width)
    scores = lax.dot_general(q, k, (((1,), (1,)), ((), ())), preferred_element_type=f32)
    top = jnp.max(scores, axis=1, keepdims=True)
    powers = jnp.exp((scores - top) * scale)
    total = jnp.sum(powers, axis=1, keepdims=True)
    weights = (powers * (1.0 / total)).astype(bf16)
    out = jnp.dot(weights, v, preferred_element_type=f32).astype(bf16)
    o_ref[...] = out.reshape(blocks, 1, rows, width)


def attend(queries, query_first, others, key_first, value_first, pairs):
    blocks, _, rows, width = queries.shape

    def spec(first):
        return pl.BlockSpec((blocks, 1, rows, width), lambda i: (0, first + i, 0, 0))

    length = blocks * rows
    return pl.pallas_call(
        attention_kernel,
        grid=(pairs,),
        in_specs=[spec(query_first), spec(key_first), spec(value_first)],
        out_specs=spec(0),
        out_shape=jax.ShapeDtypeStruct((blocks, pairs, rows, width), bf16),
        compiler_params=pltpu.CompilerParams(vmem_limit_bytes=32 * 2**20),
        cost_estimate=pl.CostEstimate(
            flops=4 * pairs * length * length * width,
            bytes_accessed=8 * pairs * length * width,
            transcendentals=pairs * length * length,
        ),
        name="attend",
    )(queries, others, others)


def choices(ids, experts):
    tokens = ids.shape[1]
    ids = jnp.concatenate([ids.astype(f32), jnp.zeros((6, tokens), f32)], axis=0).T.astype(jnp.int32)
    lanes = lax.broadcasted_iota(jnp.int32, (tokens, experts), 1)
    first = (lanes == ids[:, 0:1]).astype(f32)
    second = (lanes == ids[:, 1:2]).astype(f32)
    below = (
        lax.broadcasted_iota(jnp.int32, (tokens, tokens), 0)
        > lax.broadcasted_iota(jnp.int32, (tokens, tokens), 1)
    ).astype(bf16)
    before = jnp.dot(below, (first + second).astype(bf16), preferred_element_type=f32)
    capacity = 4 * tokens // experts
    out = []
    for k, onehot in enumerate((first, second)):
        slot = jnp.sum(before * onehot, axis=1, keepdims=True).astype(jnp.int32)
        out.append((onehot, ids[:, k : k + 1] * capacity + slot))
    return out


def placing(target, slots):
    tokens = target.shape[0]
    lanes = lax.broadcasted_iota(jnp.int32, (tokens, slots), 1)
    return (lanes == target).astype(f32).astype(bf16)


def route_kernel(
    first_ref, rest_ref, res_ref, mod_ref, router_ref, ids_ref, stream_ref, out_ref, gate_ref, tok_ref
):
    blocks, others, rows, width = rest_ref.shape
    pairs = others + 1
    seqs = mod_ref.shape[0]
    heads = blocks * pairs // seqs

    def attended(pair):
        block, place = divmod(pair, pairs)
        return (first_ref[block, 0] if place == 0 else rest_ref[block, place - 1]).astype(f32)

    experts = router_ref.shape[0]
    for b in range(seqs):
        attn = jnp.concatenate([attended(b * heads + h) for h in range(heads)], axis=1)
        mod = mod_ref[b].astype(f32)
        stream = (res_ref[b].astype(f32) + mod[0:1] * attn).astype(bf16)
        stream_ref[b * rows : (b + 1) * rows, :] = stream
        wide = stream.astype(f32)
        center = jnp.mean(wide, axis=1, keepdims=True)
        moved = wide - center
        spread = jnp.mean(moved * moved, axis=1, keepdims=True)
        tok_ref[b * rows : (b + 1) * rows, :] = (
            moved * lax.rsqrt(spread + norm_eps) * mod[1:2] + mod[2:3]
        ).astype(bf16)
    tokens = tok_ref[...]
    logits = lax.dot_general(
        tokens, router_ref[...], (((1,), (1,)), ((), ())), preferred_element_type=f32
    )
    picks = choices(ids_ref[...], experts)
    gates = [jax.nn.sigmoid(jnp.sum(onehot * logits, axis=1, keepdims=True)) for onehot, _ in picks]
    total = gates[0] + gates[1]
    gate_ref[...] = jnp.concatenate([gates[0] / total, gates[1] / total], axis=1)
    slots = out_ref.shape[0]
    place = placing(picks[0][1], slots) + placing(picks[1][1], slots)
    out_ref[...] = lax.dot_general(
        place, tokens, (((0,), (0,)), ((), ())), preferred_element_type=f32
    ).astype(bf16)


def route(first, rest, residual, modulation, router, ids):
    tokens = ids.shape[1]
    model_width = residual.shape[-1]
    slots = 4 * tokens
    return pl.pallas_call(
        route_kernel,
        out_shape=(
            jax.ShapeDtypeStruct((tokens, model_width), bf16),
            jax.ShapeDtypeStruct((slots, model_width), bf16),
            jax.ShapeDtypeStruct((tokens, 2), f32),
        ),
        scratch_shapes=[pltpu.VMEM((tokens, model_width), bf16)],
        compiler_params=pltpu.CompilerParams(vmem_limit_bytes=32 * 2**20),
        name="route",
    )(first, rest, residual, modulation, router, ids)


def combine_kernel(back_ref, stream_ref, mod_ref, gate_ref, ids_ref, out_ref, *, experts):
    seqs, rows, _ = out_ref.shape
    picks = choices(ids_ref[...], experts)
    slots = back_ref.shape[0]
    back = back_ref[...]
    moe = None
    for k in range(2):
        part = gate_ref[:, k : k + 1] * jnp.dot(
            placing(picks[k][1], slots), back, preferred_element_type=f32
        )
        moe = part if moe is None else moe + part
    for b in range(seqs):
        span = slice(b * rows, (b + 1) * rows)
        out_ref[b] = (
            stream_ref[span, :].astype(f32) + mod_ref[b, 3:4].astype(f32) * moe[span, :]
        ).astype(bf16)


def combine(back, stream, modulation, gates, ids, experts, rows):
    def kernel(*refs):
        combine_kernel(*refs, experts=experts)

    seqs = modulation.shape[0]
    return pl.pallas_call(
        kernel,
        out_shape=jax.ShapeDtypeStruct((seqs, rows, stream.shape[1]), bf16),
        compiler_params=pltpu.CompilerParams(vmem_limit_bytes=32 * 2**20),
        name="combine",
    )(back, stream, modulation, gates, ids)


def swap(blocks):
    return lax.all_to_all(blocks, "seq", split_axis=0, concat_axis=0, tiled=True)


def per_device(
    query_heads,
    key_heads,
    value_heads,
    residual,
    modulation,
    router,
    up_proj,
    down_proj,
    expert_ids,
):
    seqs_dev, head_count, len_dev, head_width = query_heads.shape
    group_indices = lax.axis_size("seq")
    pair_count = seqs_dev * head_count // group_indices
    tok_dev = seqs_dev * len_dev
    model_width = head_count * head_width
    experts = router.shape[1]
    capacity = 4 * tok_dev // experts
    ids = expert_ids.reshape(tok_dev, 2).T

    up_piece = lax.all_gather(up_proj[0], "grp", axis=0, tiled=True)
    down_piece = lax.all_gather(down_proj[0], "grp", axis=0, tiled=True)

    def arrange(array):
        return array.reshape(group_indices, pair_count, len_dev, head_width)

    def whole(queries, keys, values):
        qkv = swap(jnp.concatenate([queries, keys, values], axis=1))
        back = swap(attend(qkv, 0, qkv, pair_count, 2 * pair_count, pair_count))
        return back[:, :1], back[:, 1:]

    def pieces(queries, keys, values):
        head = swap(queries)
        body = swap(jnp.concatenate([keys, values], axis=1))
        rest = pair_count - 1
        first = swap(attend(head, 0, body, 0, pair_count, 1))
        return first, swap(attend(head, 1, body, 1, pair_count + 1, rest))

    core = lax.axis_index("grp") % 2
    first, rest = lax.cond(
        core == 0, whole, pieces, arrange(query_heads), arrange(key_heads), arrange(value_heads)
    )
    stream, outbound, gates = route(first, rest, residual, modulation, router.T, ids)
    arrived = swap(outbound.reshape(experts, capacity, model_width)).reshape(
        group_indices * capacity, model_width
    )
    pre_act = lax.dot_general(
        arrived, up_piece, (((1,), (1,)), ((), ())), preferred_element_type=f32
    )
    hidden = jax.nn.gelu(pre_act).astype(bf16)
    results = jnp.dot(hidden, down_piece, preferred_element_type=f32).astype(bf16)
    back = swap(results.reshape(group_indices, capacity, model_width)).reshape(
        experts * capacity, model_width
    )
    return combine(back, stream, modulation, gates, ids, experts, len_dev)


def solution(mesh):
    return jax.shard_map(
        per_device,
        mesh=mesh,
        in_specs=(
            P("grp", None, "seq", None),
            P("grp", None, "seq", None),
            P("grp", None, "seq", None),
            P("grp", "seq", None),
            P("grp", None, None),
            P(),
            P("seq", "grp", None),
            P("seq", "grp", None),
            P("grp", "seq", None, None),
        ),
        out_specs=P("grp", "seq", None),
        check_vma=False,
    )
```

```python
import math

import jax
import jax.numpy as jnp
from jax import lax
from jax.experimental import pallas as pl
from jax.experimental.pallas import tpu as pltpu
from jax.sharding import PartitionSpec as P

norm_eps = 1e-06
f32 = jnp.float32
bf16 = jnp.bfloat16


def attention_kernel(q_ref, k_ref, v_ref, o_ref):
    blocks, _, rows, width = q_ref.shape
    length = blocks * rows
    scale = 1.0 / math.sqrt(width)
    q = q_ref[...].reshape(length, width)
    k = k_ref[...].reshape(length, width)
    v = v_ref[...].reshape(length, width)
    scores = lax.dot_general(q, k, (((1,), (1,)), ((), ())), preferred_element_type=f32)
    top = jnp.max(scores, axis=1, keepdims=True)
    powers = jnp.exp((scores - top) * scale)
    total = jnp.sum(powers, axis=1, keepdims=True)
    weights = (powers * (1.0 / total)).astype(bf16)
    out = jnp.dot(weights, v, preferred_element_type=f32).astype(bf16)
    o_ref[...] = out.reshape(blocks, 1, rows, width)


def attend(qkv):
    blocks, triple, rows, width = qkv.shape
    pairs = triple // 3

    def spec(first):
        return pl.BlockSpec((blocks, 1, rows, width), lambda i: (0, first + i, 0, 0))

    length = blocks * rows
    return pl.pallas_call(
        attention_kernel,
        grid=(pairs,),
        in_specs=[spec(0), spec(pairs), spec(2 * pairs)],
        out_specs=spec(0),
        out_shape=jax.ShapeDtypeStruct((blocks, pairs, rows, width), bf16),
        compiler_params=pltpu.CompilerParams(vmem_limit_bytes=32 * 2**20),
        cost_estimate=pl.CostEstimate(
            flops=4 * pairs * length * length * width,
            bytes_accessed=8 * pairs * length * width,
            transcendentals=pairs * length * length,
        ),
        name="attend",
    )(qkv, qkv, qkv)


def choices(ids, experts):
    tokens = ids.shape[0]
    lanes = lax.broadcasted_iota(jnp.int32, (tokens, experts), 1)
    first = (lanes == ids[:, 0:1]).astype(f32)
    second = (lanes == ids[:, 1:2]).astype(f32)
    below = (
        lax.broadcasted_iota(jnp.int32, (tokens, tokens), 0)
        > lax.broadcasted_iota(jnp.int32, (tokens, tokens), 1)
    ).astype(bf16)
    before = jnp.dot(below, (first + second).astype(bf16), preferred_element_type=f32)
    capacity = 4 * tokens // experts
    out = []
    for k, onehot in enumerate((first, second)):
        slot = jnp.sum(before * onehot, axis=1, keepdims=True).astype(jnp.int32)
        out.append((onehot, ids[:, k : k + 1] * capacity + slot))
    return out


def placing(target, slots):
    tokens = target.shape[0]
    lanes = lax.broadcasted_iota(jnp.int32, (tokens, slots), 1)
    return (lanes == target).astype(f32).astype(bf16)


def route_kernel(attn_ref, res_ref, mod_ref, router_ref, ids_ref, stream_ref, out_ref, gate_ref, tok_ref):
    seqs, heads, rows, width = attn_ref.shape
    experts = router_ref.shape[1]
    for b in range(seqs):
        attn = jnp.concatenate([attn_ref[b, h].astype(f32) for h in range(heads)], axis=1)
        mod = mod_ref[b].astype(f32)
        stream = (res_ref[b].astype(f32) + mod[0:1] * attn).astype(bf16)
        stream_ref[b * rows : (b + 1) * rows, :] = stream
        wide = stream.astype(f32)
        center = jnp.mean(wide, axis=1, keepdims=True)
        moved = wide - center
        spread = jnp.mean(moved * moved, axis=1, keepdims=True)
        tok_ref[b * rows : (b + 1) * rows, :] = (
            moved * lax.rsqrt(spread + norm_eps) * mod[1:2] + mod[2:3]
        ).astype(bf16)
    tokens = tok_ref[...]
    logits = jnp.dot(tokens, router_ref[...], preferred_element_type=f32)
    picks = choices(ids_ref[...], experts)
    gates = [jax.nn.sigmoid(jnp.sum(onehot * logits, axis=1, keepdims=True)) for onehot, _ in picks]
    total = gates[0] + gates[1]
    gate_ref[...] = jnp.concatenate([gates[0] / total, gates[1] / total], axis=1)
    slots = out_ref.shape[0]
    place = placing(picks[0][1], slots) + placing(picks[1][1], slots)
    out_ref[...] = lax.dot_general(
        place, tokens, (((0,), (0,)), ((), ())), preferred_element_type=f32
    ).astype(bf16)


def route(attn, residual, modulation, router, ids):
    tokens = ids.shape[0]
    model_width = residual.shape[-1]
    slots = 4 * tokens
    return pl.pallas_call(
        route_kernel,
        out_shape=(
            jax.ShapeDtypeStruct((tokens, model_width), bf16),
            jax.ShapeDtypeStruct((slots, model_width), bf16),
            jax.ShapeDtypeStruct((tokens, 2), f32),
        ),
        scratch_shapes=[pltpu.VMEM((tokens, model_width), bf16)],
        compiler_params=pltpu.CompilerParams(vmem_limit_bytes=32 * 2**20),
        name="route",
    )(attn, residual, modulation, router, ids)


def combine_kernel(back_ref, stream_ref, mod_ref, gate_ref, ids_ref, out_ref, *, experts):
    seqs, rows, _ = out_ref.shape
    picks = choices(ids_ref[...], experts)
    slots = back_ref.shape[0]
    back = back_ref[...]
    moe = None
    for k in range(2):
        part = gate_ref[:, k : k + 1] * jnp.dot(
            placing(picks[k][1], slots), back, preferred_element_type=f32
        )
        moe = part if moe is None else moe + part
    for b in range(seqs):
        span = slice(b * rows, (b + 1) * rows)
        out_ref[b] = (
            stream_ref[span, :].astype(f32) + mod_ref[b, 3:4].astype(f32) * moe[span, :]
        ).astype(bf16)


def combine(back, stream, modulation, gates, ids, experts, rows):
    def kernel(*refs):
        combine_kernel(*refs, experts=experts)

    seqs = modulation.shape[0]
    return pl.pallas_call(
        kernel,
        out_shape=jax.ShapeDtypeStruct((seqs, rows, stream.shape[1]), bf16),
        compiler_params=pltpu.CompilerParams(vmem_limit_bytes=32 * 2**20),
        name="combine",
    )(back, stream, modulation, gates, ids)


def mlp_kernel(x_ref, up_ref, down_ref, o_ref, pre_ref, acc_ref):
    step = pl.program_id(0)
    last = pl.num_programs(0) - 1

    def ahead():
        return lax.dot_general(
            x_ref[...], up_ref[...], (((1,), (1,)), ((), ())), preferred_element_type=f32
        )

    def behind():
        hidden = jax.nn.gelu(pre_ref[...]).astype(bf16)
        return jnp.dot(hidden, down_ref[...], preferred_element_type=f32)

    @pl.when(step == 0)
    def _():
        pre_ref[...] = ahead()

    @pl.when(step == 1)
    def _():
        part, pre = behind(), ahead()
        acc_ref[...] = part
        pre_ref[...] = pre

    @pl.when((step > 1) & (step < last))
    def _():
        part, pre = behind(), ahead()
        acc_ref[...] += part
        pre_ref[...] = pre

    @pl.when(step == last)
    def _():
        o_ref[...] = (acc_ref[...] + behind()).astype(bf16)


def mlp(rows, up, down, tile):
    count, width = rows.shape
    tiles = up.shape[0] // tile
    return pl.pallas_call(
        mlp_kernel,
        grid=(tiles + 1,),
        in_specs=[
            pl.BlockSpec((count, width), lambda i: (0, 0)),
            pl.BlockSpec((tile, width), lambda i: (jnp.minimum(i, tiles - 1), 0)),
            pl.BlockSpec((tile, width), lambda i: (jnp.maximum(i - 1, 0), 0)),
        ],
        out_specs=pl.BlockSpec((count, width), lambda i: (0, 0)),
        out_shape=jax.ShapeDtypeStruct((count, width), bf16),
        scratch_shapes=[pltpu.VMEM((count, tile), f32), pltpu.VMEM((count, width), f32)],
        compiler_params=pltpu.CompilerParams(vmem_limit_bytes=46 * 2**20),
        cost_estimate=pl.CostEstimate(
            flops=4 * count * width * up.shape[0],
            bytes_accessed=4 * width * (count + up.shape[0]),
            transcendentals=count * up.shape[0],
        ),
        name="mlp",
    )(rows, up, down)


def swap(blocks):
    return lax.all_to_all(blocks, "seq", split_axis=0, concat_axis=0, tiled=True)


def per_device(
    query_heads,
    key_heads,
    value_heads,
    residual,
    modulation,
    router,
    up_proj,
    down_proj,
    expert_ids,
):
    seqs_dev, head_count, len_dev, head_width = query_heads.shape
    group_indices = lax.axis_size("seq")
    pair_count = seqs_dev * head_count // group_indices
    tok_dev = seqs_dev * len_dev
    model_width = head_count * head_width
    experts = router.shape[1]
    capacity = 4 * tok_dev // experts
    ids = expert_ids.reshape(tok_dev, 2)

    up_piece = lax.all_gather(up_proj[0], "grp", axis=0, tiled=True)
    down_piece = lax.all_gather(down_proj[0], "grp", axis=0, tiled=True)

    def arrange(array):
        return array.reshape(group_indices, pair_count, len_dev, head_width)

    def together(*arrays):
        return swap(jnp.concatenate(arrays, axis=1))

    def apart(*arrays):
        parts = [swap(arrays[0]), swap(jnp.concatenate(arrays[1:], axis=1))]
        return jnp.concatenate(parts, axis=1)

    core = lax.axis_index("grp") % 2
    qkv = lax.cond(
        core == 0, together, apart, arrange(query_heads), arrange(key_heads), arrange(value_heads)
    )
    def by_pair(pairs):
        return jnp.concatenate([swap(pairs[:, :1]), swap(pairs[:, 1:])], axis=1)

    attn = lax.cond(core == 0, swap, by_pair, attend(qkv)).reshape(
        seqs_dev, head_count, len_dev, head_width
    )
    stream, outbound, gates = route(attn, residual, modulation, router, ids)
    arrived = swap(outbound.reshape(experts, capacity, model_width)).reshape(
        group_indices * capacity, model_width
    )
    results = mlp(arrived, up_piece, down_piece, 4 * up_proj.shape[1])
    back = swap(results.reshape(group_indices, capacity, model_width)).reshape(
        experts * capacity, model_width
    )
    return combine(back, stream, modulation, gates, ids, experts, len_dev)


def solution(mesh):
    return jax.shard_map(
        per_device,
        mesh=mesh,
        in_specs=(
            P("grp", None, "seq", None),
            P("grp", None, "seq", None),
            P("grp", None, "seq", None),
            P("grp", "seq", None),
            P("grp", None, None),
            P(),
            P("seq", "grp", None),
            P("seq", "grp", None),
            P("grp", "seq", None, None),
        ),
        out_specs=P("grp", "seq", None),
        check_vma=False,
    )
```

```python
import math

import jax
import jax.numpy as jnp
from jax import lax
from jax.experimental import pallas as pl
from jax.experimental.pallas import tpu as pltpu
from jax.sharding import PartitionSpec as P

norm_eps = 1e-06
f32 = jnp.float32
bf16 = jnp.bfloat16


def attention_kernel(qkv_ref, o_ref):
    blocks, pairs, rows, width = o_ref.shape
    length = blocks * rows
    scale = 1.0 / math.sqrt(width)
    for i in range(pairs):
        q, k, v = (qkv_ref[:, i + kind * pairs].reshape(length, width) for kind in range(3))
        scores = lax.dot_general(q, k, (((1,), (1,)), ((), ())), preferred_element_type=f32)
        top = jnp.max(scores, axis=1, keepdims=True)
        powers = jnp.exp((scores - top) * scale)
        total = jnp.sum(powers, axis=1, keepdims=True)
        out = jnp.dot(powers.astype(bf16), v, preferred_element_type=f32) * (1.0 / total)
        o_ref[:, i] = out.astype(bf16).reshape(blocks, rows, width)


def attend(qkv):
    blocks, triple, rows, width = qkv.shape
    pairs = triple // 3
    length = blocks * rows
    return pl.pallas_call(
        attention_kernel,
        out_shape=jax.ShapeDtypeStruct((blocks, pairs, rows, width), bf16),
        compiler_params=pltpu.CompilerParams(vmem_limit_bytes=32 * 2**20),
        cost_estimate=pl.CostEstimate(
            flops=4 * pairs * length * length * width,
            bytes_accessed=8 * pairs * length * width,
            transcendentals=pairs * length * length,
        ),
        name="attend",
    )(qkv)


def choices(ids, experts):
    tokens = ids.shape[0]
    lanes = lax.broadcasted_iota(jnp.int32, (tokens, experts), 1)
    first = (lanes == ids[:, 0:1]).astype(f32)
    second = (lanes == ids[:, 1:2]).astype(f32)
    below = (
        lax.broadcasted_iota(jnp.int32, (tokens, tokens), 0)
        > lax.broadcasted_iota(jnp.int32, (tokens, tokens), 1)
    ).astype(bf16)
    before = jnp.dot(below, (first + second).astype(bf16), preferred_element_type=f32)
    capacity = 4 * tokens // experts
    out = []
    for k, onehot in enumerate((first, second)):
        slot = jnp.sum(before * onehot, axis=1, keepdims=True).astype(jnp.int32)
        out.append((onehot, ids[:, k : k + 1] * capacity + slot))
    return out


def placing(target, slots):
    tokens = target.shape[0]
    lanes = lax.broadcasted_iota(jnp.int32, (tokens, slots), 1)
    return (lanes == target).astype(f32).astype(bf16)


def route_kernel(attn_ref, res_ref, mod_ref, router_ref, ids_ref, stream_ref, out_ref, gate_ref, tok_ref):
    seqs, heads, rows, width = attn_ref.shape
    experts = router_ref.shape[1]
    for b in range(seqs):
        attn = jnp.concatenate([attn_ref[b, h].astype(f32) for h in range(heads)], axis=1)
        mod = mod_ref[b].astype(f32)
        stream = (res_ref[b].astype(f32) + mod[0:1] * attn).astype(bf16)
        stream_ref[b * rows : (b + 1) * rows, :] = stream
        wide = stream.astype(f32)
        center = jnp.mean(wide, axis=1, keepdims=True)
        moved = wide - center
        spread = jnp.mean(moved * moved, axis=1, keepdims=True)
        tok_ref[b * rows : (b + 1) * rows, :] = (
            moved * lax.rsqrt(spread + norm_eps) * mod[1:2] + mod[2:3]
        ).astype(bf16)
    tokens = tok_ref[...]
    logits = jnp.dot(tokens, router_ref[...], preferred_element_type=f32)
    picks = choices(ids_ref[...], experts)
    gates = [jax.nn.sigmoid(jnp.sum(onehot * logits, axis=1, keepdims=True)) for onehot, _ in picks]
    total = gates[0] + gates[1]
    gate_ref[...] = jnp.concatenate([gates[0] / total, gates[1] / total], axis=1)
    slots = out_ref.shape[0]
    place = placing(picks[0][1], slots) + placing(picks[1][1], slots)
    out_ref[...] = lax.dot_general(
        place, tokens, (((0,), (0,)), ((), ())), preferred_element_type=f32
    ).astype(bf16)


def route(attn, residual, modulation, router, ids):
    tokens = ids.shape[0]
    model_width = residual.shape[-1]
    slots = 4 * tokens
    return pl.pallas_call(
        route_kernel,
        out_shape=(
            jax.ShapeDtypeStruct((tokens, model_width), bf16),
            jax.ShapeDtypeStruct((slots, model_width), bf16),
            jax.ShapeDtypeStruct((tokens, 2), f32),
        ),
        scratch_shapes=[pltpu.VMEM((tokens, model_width), bf16)],
        compiler_params=pltpu.CompilerParams(vmem_limit_bytes=32 * 2**20),
        name="route",
    )(attn, residual, modulation, router, ids)


def combine_kernel(back_ref, stream_ref, mod_ref, gate_ref, ids_ref, out_ref, *, experts):
    seqs, rows, _ = out_ref.shape
    picks = choices(ids_ref[...], experts)
    slots = back_ref.shape[0]
    back = back_ref[...]
    tokens = stream_ref.shape[0]
    place = jnp.concatenate([placing(target, slots) for _, target in picks], axis=0)
    fetched = jnp.dot(place, back, preferred_element_type=f32)
    moe = gate_ref[:, 0:1] * fetched[:tokens] + gate_ref[:, 1:2] * fetched[tokens:]
    for b in range(seqs):
        span = slice(b * rows, (b + 1) * rows)
        out_ref[b] = (
            stream_ref[span, :].astype(f32) + mod_ref[b, 3:4].astype(f32) * moe[span, :]
        ).astype(bf16)


def combine(back, stream, modulation, gates, ids, experts, rows):
    def kernel(*refs):
        combine_kernel(*refs, experts=experts)

    seqs = modulation.shape[0]
    return pl.pallas_call(
        kernel,
        out_shape=jax.ShapeDtypeStruct((seqs, rows, stream.shape[1]), bf16),
        compiler_params=pltpu.CompilerParams(vmem_limit_bytes=32 * 2**20),
        name="combine",
    )(back, stream, modulation, gates, ids)


def mlp_kernel(x_ref, up_ref, down_ref, o_ref, pre_ref, acc_ref):
    step = pl.program_id(0)
    last = pl.num_programs(0) - 1

    def ahead():
        return lax.dot_general(
            x_ref[...], up_ref[...], (((1,), (1,)), ((), ())), preferred_element_type=f32
        )

    def behind():
        hidden = jax.nn.gelu(pre_ref[...]).astype(bf16)
        return jnp.dot(hidden, down_ref[...], preferred_element_type=f32)

    @pl.when(step == 0)
    def _():
        pre_ref[...] = ahead()

    @pl.when(step == 1)
    def _():
        part, pre = behind(), ahead()
        acc_ref[...] = part
        pre_ref[...] = pre

    @pl.when((step > 1) & (step < last))
    def _():
        part, pre = behind(), ahead()
        acc_ref[...] += part
        pre_ref[...] = pre

    @pl.when(step == last)
    def _():
        o_ref[...] = (acc_ref[...] + behind()).astype(bf16)


def mlp(rows, up, down, tile):
    count, width = rows.shape
    tiles = up.shape[0] // tile
    return pl.pallas_call(
        mlp_kernel,
        grid=(tiles + 1,),
        in_specs=[
            pl.BlockSpec((count, width), lambda i: (0, 0)),
            pl.BlockSpec((tile, width), lambda i: (jnp.minimum(i, tiles - 1), 0)),
            pl.BlockSpec((tile, width), lambda i: (jnp.maximum(i - 1, 0), 0)),
        ],
        out_specs=pl.BlockSpec((count, width), lambda i: (0, 0)),
        out_shape=jax.ShapeDtypeStruct((count, width), bf16),
        scratch_shapes=[pltpu.VMEM((count, tile), f32), pltpu.VMEM((count, width), f32)],
        compiler_params=pltpu.CompilerParams(vmem_limit_bytes=46 * 2**20),
        cost_estimate=pl.CostEstimate(
            flops=4 * count * width * up.shape[0],
            bytes_accessed=4 * width * (count + up.shape[0]),
            transcendentals=count * up.shape[0],
        ),
        name="mlp",
    )(rows, up, down)


def swap(blocks):
    return lax.all_to_all(blocks, "seq", split_axis=0, concat_axis=0, tiled=True)


def per_device(
    query_heads,
    key_heads,
    value_heads,
    residual,
    modulation,
    router,
    up_proj,
    down_proj,
    expert_ids,
):
    seqs_dev, head_count, len_dev, head_width = query_heads.shape
    group_indices = lax.axis_size("seq")
    pair_count = seqs_dev * head_count // group_indices
    tok_dev = seqs_dev * len_dev
    model_width = head_count * head_width
    experts = router.shape[1]
    capacity = 4 * tok_dev // experts
    ids = expert_ids.reshape(tok_dev, 2)

    up_piece = lax.all_gather(up_proj[0], "grp", axis=0, tiled=True)
    down_piece = lax.all_gather(down_proj[0], "grp", axis=0, tiled=True)

    def arrange(array):
        return array.reshape(group_indices, pair_count, len_dev, head_width)

    def together(*arrays):
        return swap(jnp.concatenate(arrays, axis=1))

    def apart(*arrays):
        parts = [swap(arrays[0]), swap(jnp.concatenate(arrays[1:], axis=1))]
        return jnp.concatenate(parts, axis=1)

    core = lax.axis_index("grp") % 2
    qkv = lax.cond(
        core == 0, together, apart, arrange(query_heads), arrange(key_heads), arrange(value_heads)
    )
    def by_pair(pairs):
        return jnp.concatenate([swap(pairs[:, :1]), swap(pairs[:, 1:])], axis=1)

    attn = lax.cond(core == 0, swap, by_pair, attend(qkv)).reshape(
        seqs_dev, head_count, len_dev, head_width
    )
    stream, outbound, gates = route(attn, residual, modulation, router, ids)
    arrived = swap(outbound.reshape(experts, capacity, model_width)).reshape(
        group_indices * capacity, model_width
    )
    results = mlp(arrived, up_piece, down_piece, 4 * up_proj.shape[1])
    back = swap(results.reshape(group_indices, capacity, model_width)).reshape(
        experts * capacity, model_width
    )
    return combine(back, stream, modulation, gates, ids, experts, len_dev)


def solution(mesh):
    return jax.shard_map(
        per_device,
        mesh=mesh,
        in_specs=(
            P("grp", None, "seq", None),
            P("grp", None, "seq", None),
            P("grp", None, "seq", None),
            P("grp", "seq", None),
            P("grp", None, None),
            P(),
            P("seq", "grp", None),
            P("seq", "grp", None),
            P("grp", "seq", None, None),
        ),
        out_specs=P("grp", "seq", None),
        check_vma=False,
    )
```

```python
import math

import jax
import jax.numpy as jnp
from jax import lax
from jax.experimental import pallas as pl
from jax.experimental.pallas import tpu as pltpu
from jax.sharding import PartitionSpec as P

norm_eps = 1e-06
f32 = jnp.float32
bf16 = jnp.bfloat16


def attention_kernel(qkv_ref, first_ref, rest_ref):
    blocks, others, rows, width = rest_ref.shape
    pairs = others + 1
    length = blocks * rows
    scale = 1.0 / math.sqrt(width)
    for i in range(pairs):
        q, k, v = (qkv_ref[:, i + kind * pairs].reshape(length, width) for kind in range(3))
        scores = lax.dot_general(q, k, (((1,), (1,)), ((), ())), preferred_element_type=f32)
        top = jnp.max(scores, axis=1, keepdims=True)
        powers = jnp.exp((scores - top) * scale)
        total = jnp.sum(powers, axis=1, keepdims=True)
        out = jnp.dot(powers.astype(bf16), v, preferred_element_type=f32) * (1.0 / total)
        ref, place = (first_ref, 0) if i == 0 else (rest_ref, i - 1)
        ref[:, place] = out.astype(bf16).reshape(blocks, rows, width)


def attend(qkv):
    blocks, triple, rows, width = qkv.shape
    pairs = triple // 3
    length = blocks * rows
    return pl.pallas_call(
        attention_kernel,
        out_shape=tuple(
            jax.ShapeDtypeStruct((blocks, part, rows, width), bf16) for part in (1, pairs - 1)
        ),
        compiler_params=pltpu.CompilerParams(vmem_limit_bytes=32 * 2**20),
        cost_estimate=pl.CostEstimate(
            flops=4 * pairs * length * length * width,
            bytes_accessed=8 * pairs * length * width,
            transcendentals=pairs * length * length,
        ),
        name="attend",
    )(qkv)


def choices(ids, experts):
    tokens = ids.shape[0]
    lanes = lax.broadcasted_iota(jnp.int32, (tokens, experts), 1)
    first = (lanes == ids[:, 0:1]).astype(f32)
    second = (lanes == ids[:, 1:2]).astype(f32)
    below = (
        lax.broadcasted_iota(jnp.int32, (tokens, tokens), 0)
        > lax.broadcasted_iota(jnp.int32, (tokens, tokens), 1)
    ).astype(bf16)
    before = jnp.dot(below, (first + second).astype(bf16), preferred_element_type=f32)
    capacity = 4 * tokens // experts
    out = []
    for k, onehot in enumerate((first, second)):
        slot = jnp.sum(before * onehot, axis=1, keepdims=True).astype(jnp.int32)
        out.append((onehot, ids[:, k : k + 1] * capacity + slot))
    return out


def placing(target, slots):
    tokens = target.shape[0]
    lanes = lax.broadcasted_iota(jnp.int32, (tokens, slots), 1)
    return (lanes == target).astype(f32).astype(bf16)


def route_kernel(attn_ref, res_ref, mod_ref, router_ref, ids_ref, stream_ref, out_ref, gate_ref, tok_ref):
    seqs, heads, rows, width = attn_ref.shape
    experts = router_ref.shape[1]
    for b in range(seqs):
        attn = jnp.concatenate([attn_ref[b, h].astype(f32) for h in range(heads)], axis=1)
        mod = mod_ref[b].astype(f32)
        stream = (res_ref[b].astype(f32) + mod[0:1] * attn).astype(bf16)
        stream_ref[b * rows : (b + 1) * rows, :] = stream
        wide = stream.astype(f32)
        center = jnp.mean(wide, axis=1, keepdims=True)
        moved = wide - center
        spread = jnp.mean(moved * moved, axis=1, keepdims=True)
        tok_ref[b * rows : (b + 1) * rows, :] = (
            moved * lax.rsqrt(spread + norm_eps) * mod[1:2] + mod[2:3]
        ).astype(bf16)
    tokens = tok_ref[...]
    logits = jnp.dot(tokens, router_ref[...], preferred_element_type=f32)
    picks = choices(ids_ref[...], experts)
    gates = [jax.nn.sigmoid(jnp.sum(onehot * logits, axis=1, keepdims=True)) for onehot, _ in picks]
    total = gates[0] + gates[1]
    gate_ref[...] = jnp.concatenate([gates[0] / total, gates[1] / total], axis=1)
    slots = out_ref.shape[0]
    place = placing(picks[0][1], slots) + placing(picks[1][1], slots)
    out_ref[...] = lax.dot_general(
        place, tokens, (((0,), (0,)), ((), ())), preferred_element_type=f32
    ).astype(bf16)


def route(attn, residual, modulation, router, ids):
    tokens = ids.shape[0]
    model_width = residual.shape[-1]
    slots = 4 * tokens
    return pl.pallas_call(
        route_kernel,
        out_shape=(
            jax.ShapeDtypeStruct((tokens, model_width), bf16),
            jax.ShapeDtypeStruct((slots, model_width), bf16),
            jax.ShapeDtypeStruct((tokens, 2), f32),
        ),
        scratch_shapes=[pltpu.VMEM((tokens, model_width), bf16)],
        compiler_params=pltpu.CompilerParams(vmem_limit_bytes=32 * 2**20),
        name="route",
    )(attn, residual, modulation, router, ids)


def combine_kernel(back_ref, stream_ref, mod_ref, gate_ref, ids_ref, out_ref, *, experts):
    seqs, rows, _ = out_ref.shape
    picks = choices(ids_ref[...], experts)
    slots = back_ref.shape[0]
    back = back_ref[...]
    tokens = stream_ref.shape[0]
    place = jnp.concatenate([placing(target, slots) for _, target in picks], axis=0)
    fetched = jnp.dot(place, back, preferred_element_type=f32)
    moe = gate_ref[:, 0:1] * fetched[:tokens] + gate_ref[:, 1:2] * fetched[tokens:]
    for b in range(seqs):
        span = slice(b * rows, (b + 1) * rows)
        out_ref[b] = (
            stream_ref[span, :].astype(f32) + mod_ref[b, 3:4].astype(f32) * moe[span, :]
        ).astype(bf16)


def combine(back, stream, modulation, gates, ids, experts, rows):
    def kernel(*refs):
        combine_kernel(*refs, experts=experts)

    seqs = modulation.shape[0]
    return pl.pallas_call(
        kernel,
        out_shape=jax.ShapeDtypeStruct((seqs, rows, stream.shape[1]), bf16),
        compiler_params=pltpu.CompilerParams(vmem_limit_bytes=32 * 2**20),
        name="combine",
    )(back, stream, modulation, gates, ids)


def mlp_kernel(x_ref, up_ref, down_ref, o_ref, pre_ref, acc_ref):
    step = pl.program_id(0)
    last = pl.num_programs(0) - 1

    def ahead():
        return lax.dot_general(
            x_ref[...], up_ref[...], (((1,), (1,)), ((), ())), preferred_element_type=f32
        )

    def behind():
        hidden = jax.nn.gelu(pre_ref[...]).astype(bf16)
        return jnp.dot(hidden, down_ref[...], preferred_element_type=f32)

    @pl.when(step == 0)
    def _():
        pre_ref[...] = ahead()

    @pl.when(step == 1)
    def _():
        part, pre = behind(), ahead()
        acc_ref[...] = part
        pre_ref[...] = pre

    @pl.when((step > 1) & (step < last))
    def _():
        part, pre = behind(), ahead()
        acc_ref[...] += part
        pre_ref[...] = pre

    @pl.when(step == last)
    def _():
        o_ref[...] = (acc_ref[...] + behind()).astype(bf16)


def mlp(rows, up, down, tile):
    count, width = rows.shape
    tiles = up.shape[0] // tile
    return pl.pallas_call(
        mlp_kernel,
        grid=(tiles + 1,),
        in_specs=[
            pl.BlockSpec((count, width), lambda i: (0, 0)),
            pl.BlockSpec((tile, width), lambda i: (jnp.minimum(i, tiles - 1), 0)),
            pl.BlockSpec((tile, width), lambda i: (jnp.maximum(i - 1, 0), 0)),
        ],
        out_specs=pl.BlockSpec((count, width), lambda i: (0, 0)),
        out_shape=jax.ShapeDtypeStruct((count, width), bf16),
        scratch_shapes=[pltpu.VMEM((count, tile), f32), pltpu.VMEM((count, width), f32)],
        compiler_params=pltpu.CompilerParams(vmem_limit_bytes=46 * 2**20),
        cost_estimate=pl.CostEstimate(
            flops=4 * count * width * up.shape[0],
            bytes_accessed=4 * width * (count + up.shape[0]),
            transcendentals=count * up.shape[0],
        ),
        name="mlp",
    )(rows, up, down)


def swap(blocks):
    return lax.all_to_all(blocks, "seq", split_axis=0, concat_axis=0, tiled=True)


def per_device(
    query_heads,
    key_heads,
    value_heads,
    residual,
    modulation,
    router,
    up_proj,
    down_proj,
    expert_ids,
):
    seqs_dev, head_count, len_dev, head_width = query_heads.shape
    group_indices = lax.axis_size("seq")
    pair_count = seqs_dev * head_count // group_indices
    tok_dev = seqs_dev * len_dev
    model_width = head_count * head_width
    experts = router.shape[1]
    capacity = 4 * tok_dev // experts
    ids = expert_ids.reshape(tok_dev, 2)

    up_piece = lax.all_gather(up_proj[0], "grp", axis=0, tiled=True)
    down_piece = lax.all_gather(down_proj[0], "grp", axis=0, tiled=True)

    def arrange(array):
        return array.reshape(group_indices, pair_count, len_dev, head_width)

    def together(*arrays):
        return swap(jnp.concatenate(arrays, axis=1))

    def apart(*arrays):
        parts = [swap(arrays[0]), swap(jnp.concatenate(arrays[1:], axis=1))]
        return jnp.concatenate(parts, axis=1)

    core = lax.axis_index("grp") % 2
    qkv = lax.cond(
        core == 0, together, apart, arrange(query_heads), arrange(key_heads), arrange(value_heads)
    )
    def at_once(first, rest):
        return swap(jnp.concatenate([first, rest], axis=1))

    def by_pair(first, rest):
        return jnp.concatenate([swap(first), swap(rest)], axis=1)

    attn = lax.cond(core == 0, at_once, by_pair, *attend(qkv)).reshape(
        seqs_dev, head_count, len_dev, head_width
    )
    stream, outbound, gates = route(attn, residual, modulation, router, ids)
    arrived = swap(outbound.reshape(experts, capacity, model_width)).reshape(
        group_indices * capacity, model_width
    )
    results = mlp(arrived, up_piece, down_piece, 4 * up_proj.shape[1])
    back = swap(results.reshape(group_indices, capacity, model_width)).reshape(
        experts * capacity, model_width
    )
    return combine(back, stream, modulation, gates, ids, experts, len_dev)


def solution(mesh):
    return jax.shard_map(
        per_device,
        mesh=mesh,
        in_specs=(
            P("grp", None, "seq", None),
            P("grp", None, "seq", None),
            P("grp", None, "seq", None),
            P("grp", "seq", None),
            P("grp", None, None),
            P(),
            P("seq", "grp", None),
            P("seq", "grp", None),
            P("grp", "seq", None, None),
        ),
        out_specs=P("grp", "seq", None),
        check_vma=False,
    )
```
